128 devices in a mesh: row: 8 (over y, x_lo), col: 16 (over x_hi, z, core).
Axes of the slice: x: 4 (x_hi: 2, x_lo: 2; x = x_hi * 2 + x_lo), y: 4, z: 4, core: 2. Of those that a mesh axis runs over, the one named last changes fastest.
Arguments:
- segments: float32 [49152, 512], P(('row', 'col')), may hold values from -60 to 60
- exclusion: int32 [1], replicated, may hold values from 1 to 12
Outputs:
- profile: float32 [2, 49152], P(None, ('row', 'col'))
The draws below stay inside these ranges and needn't reach their ends.
All inputs are finite; a program needn't handle non-finite values.
Results may differ from the reference program's by a relative error of at most 0.0005.
Values may be sent and summed in bfloat16 or wider, within the bound.
No kernel may reach another device: no remote copies, remote signals or barrier semaphores. Data moves between devices by JAX's collectives and lax.ppermute only.
A program may use at most 192 MiB of HBM per device.

```python
import math
import jax
import jax.numpy as jnp
from jax import lax

SEG_LEN = 512
SEG_DEV = 384
NSEG = 49152


def draw_segments(key, part):
    key = jax.random.fold_in(key, 11)
    subkeys = jax.random.split(key, 7)
    pair_count = NSEG // 2
    shuffle = jax.random.permutation(subkeys[0], NSEG)
    pair_id = jnp.zeros((NSEG,), jnp.int32).at[shuffle].set(jnp.arange(NSEG, dtype=jnp.int32) // 2)
    motifs = jax.random.normal(subkeys[1], (pair_count, SEG_LEN), jnp.float32)
    drawn_fresh = jax.random.normal(subkeys[2], (NSEG + 15, SEG_LEN), jnp.float32)
    jitter = 0.5 * jax.random.normal(subkeys[4], (NSEG, SEG_LEN), jnp.float32)
    amp_low, amp_high = (0.2, 3.0)
    strength = jnp.exp(jax.random.uniform(subkeys[3], (pair_count,), jnp.float32, math.log(amp_low), math.log(amp_high)))
    nearby = drawn_fresh[0:NSEG]
    for shift_by in range(1, 16):
        nearby = nearby + drawn_fresh[shift_by:shift_by + NSEG]
    nearby = 0.25 * nearby
    signal = strength[pair_id][:, None] * motifs[pair_id] + nearby + jitter
    offset_lvl = 3.0 * jax.random.normal(subkeys[5], (NSEG, 1), jnp.float32)
    factor = jnp.exp(jax.random.uniform(subkeys[6], (NSEG, 1), jnp.float32, math.log(0.5), math.log(4.0)))
    return jnp.clip(offset_lvl + factor * signal, -60.0, 60.0)


def setup_inputs(seed: int = 0) -> dict:
    seeds = jax.random.split(jax.random.key(seed), 3)
    segments = draw_segments(jax.random.fold_in(seeds[2], 71), 0)
    exclusion = jax.random.randint(seeds[1], (1,), 1, 13).astype(jnp.int32)
    return {"segments": segments, "exclusion": exclusion}


def statistics(segments):
    seg_len = segments.shape[1]
    average = lax.optimization_barrier(jnp.mean(segments, axis=1))
    centered = segments - average[:, None]
    spread_inv = lax.rsqrt(lax.optimization_barrier(jnp.mean(centered * centered, axis=1)) + 1e-05) * (1.0 / math.sqrt(seg_len))
    return (average, spread_inv)

def normalize(samples, average, spread_inv):
    return ((samples - average[:, None]) * spread_inv[:, None]).astype(jnp.bfloat16)

def reference(segments, exclusion):
    average, spread_inv = statistics(segments)
    normed = normalize(segments, average, spread_inv)
    exclude = exclusion[0]
    row_count = 2 * SEG_DEV
    positions = jnp.arange(NSEG, dtype=jnp.int32)

    def row_minima(blk_index):
        begin_at = (blk_index * row_count).astype(jnp.int32)
        row_data = lax.dynamic_slice_in_dim(normed, begin_at, row_count, 0)
        products = jnp.dot(row_data, normed.T, preferred_element_type=jnp.float32)
        row_pos = begin_at + jnp.arange(row_count, dtype=jnp.int32)
        offset_by = positions[None, :] - row_pos[:, None]
        later = lax.optimization_barrier(jnp.min(jnp.where(offset_by > exclude, 1.0 - products, 4.0), axis=1))
        earlier = lax.optimization_barrier(jnp.min(jnp.where(offset_by < -exclude, 1.0 - products, 4.0), axis=1))
        return jnp.stack([earlier, later])
    minima = lax.map(row_minima, jnp.arange(NSEG // row_count, dtype=jnp.int32))
    return jnp.transpose(minima, (1, 0, 2)).reshape(2, NSEG)
```

```python
import functools
import math

import jax
import jax.numpy as jnp
import numpy as np
from jax import lax
from jax.experimental import pallas as pl
from jax.experimental.pallas import tpu as pltpu
from jax.sharding import PartitionSpec as P

AXES = ("row", "col")
SIDE = 4
OFFSETS = (
    ((3, 3, 0), (0, 1, 0)),
    ((1, 0, 3), (0, 0, 1)),
    ((0, 0, 3), (1, 1, 0)),
    ((3, 3, 3), (0, 2, 1)),
    ((2, 0, 3), (0, 3, 1)),
)
SOURCES = (None, None, None, 0, 1)
SLOTS = ((0, 0, 0),) + tuple(off for pair in OFFSETS for off in pair)
LOW = -3.0


def coords(device):
    row, col = divmod(device, 16)
    y, x_lo = divmod(row, 2)
    return (col // 8 * 2 + x_lo, y, col // 2 % SIDE, col % 2)


def device_at(x, y, z, core):
    x, y, z = x % SIDE, y % SIDE, z % SIDE
    return (y * 2 + x % 2) * 16 + x // 2 * 8 + z * 2 + core


def minus(a, b):
    return tuple((p - q) % SIDE for p, q in zip(a, b))


def moves(hops):
    out = []
    for target in range(128):
        x, y, z, core = coords(target)
        dx, dy, dz = hops[core]
        out.append((device_at(x + dx, y + dy, z + dz, core), target))
    return out


def across():
    return [(device, device ^ 1) for device in range(128)]


def pair_lists():
    chosen = {}
    for t in range(len(SLOTS)):
        for s in range(t):
            diff = minus(SLOTS[t], SLOTS[s])
            key = min(diff, minus((0, 0, 0), diff))
            if key not in chosen:
                chosen[key] = (s, t)
    assert len(chosen) == 35
    full, half = [], []
    for key, pair in chosen.items():
        (half if key == minus((0, 0, 0), key) else full).append(pair)
    return full, half


def normalize_kernel(x_ref, o_ref):
    x = x_ref[...]
    length = x.shape[1]
    average = jnp.sum(x, axis=1, keepdims=True) * (1.0 / length)
    centered = x - average
    power = jnp.sum(centered * centered, axis=1, keepdims=True) * (1.0 / length)
    spread_inv = lax.rsqrt(power + 1e-05) * (1.0 / math.sqrt(length))
    o_ref[...] = (centered * spread_inv).astype(jnp.bfloat16)


def phase_kernel(n_moved, groups, diag, has_prev, rows, *refs):
    meta, table = refs[:2]
    blocks = refs[2 : 3 + 2 * n_moved]
    rest = refs[3 + 2 * n_moved :]
    prev = rest[0] if has_prev else None
    rest = rest[1:] if has_prev else rest
    out, data, row_acc, col_acc, sems = rest
    core = meta[0]
    exclude = meta[1]

    def copies(index):
        if index == 0:
            slot, first = 0, core
        else:
            first = core if index % 2 else 1 - core
            slot = 1 + (index - 1) // 2 * 2 + first
        base = slot * 2 * rows
        near = pl.multiple_of(base + first * rows, rows)
        far = pl.multiple_of(base + (1 - first) * rows, rows)
        return (
            pltpu.make_async_copy(
                blocks[index].at[pl.ds(0, rows)], data.at[pl.ds(near, rows)], sems.at[index, 0]
            ),
            pltpu.make_async_copy(
                blocks[index].at[pl.ds(rows, rows)], data.at[pl.ds(far, rows)], sems.at[index, 1]
            ),
        )

    for index in range(len(blocks)):
        for copy in copies(index):
            copy.start()

    row_acc[...] = jnp.full(row_acc.shape, LOW, jnp.float32)
    col_acc[...] = jnp.full(col_acc.shape, LOW, jnp.float32)

    def product(a, start, width):
        b = data[pl.ds(pl.multiple_of(start, 128), width), :]
        return lax.dot_general(
            a, b, (((1,), (1,)), ((), ())), preferred_element_type=jnp.float32
        )

    def row_max(values):
        best = values[:, :128]
        for at in range(128, values.shape[1], 128):
            best = jnp.maximum(best, values[:, at : at + 128])
        return best

    def col_max(values):
        return jnp.max(values.reshape(rows // 8, 8, values.shape[1]), axis=0)

    def row_block(slot):
        return data[pl.ds(pl.multiple_of((2 * slot + core) * rows, rows), rows), :]

    def visit(index, carry):
        s = table[2 * index]
        t = table[2 * index + 1]
        order_s = meta[2 + s]
        order_t = meta[2 + t]
        later = (order_t > order_s).astype(jnp.int32)
        row_at = 2 * s + later
        col_at = 2 * t + 1 - later
        near = jnp.abs(order_t - order_s) == 1

        def run(masked):
            a = row_block(s)
            best = row_acc[row_at]
            for part in range(2 * rows // 256):
                values = product(a, 2 * t * rows + part * 256, 256)
                if masked:
                    first = (order_t - order_s) * 2 * rows + part * 256 - core * rows
                    offset = (
                        lax.broadcasted_iota(jnp.int32, values.shape, 1)
                        - lax.broadcasted_iota(jnp.int32, values.shape, 0)
                        + first
                    )
                    values = jnp.where(jnp.abs(offset) > exclude, values, LOW)
                best = jnp.maximum(best, row_max(values))
                at = pl.ds(part * 256, 256)
                col_acc[col_at, :, at] = jnp.maximum(col_acc[col_at, :, at], col_max(values))
            row_acc[row_at] = best

        pl.when(near)(functools.partial(run, True))
        pl.when(jnp.logical_not(near))(functools.partial(run, False))
        return carry

    def visit_half(index, carry):
        s = table[2 * index]
        t = table[2 * index + 1]
        later = (meta[2 + t] > meta[2 + s]).astype(jnp.int32)
        row_at = 2 * s + later
        col_at = 2 * t + 1 - later
        half = jnp.where(later == 1, core, 1 - core)
        values = product(row_block(s), (2 * t + half) * rows, rows)
        row_acc[row_at] = jnp.maximum(row_acc[row_at], row_max(values))
        at = pl.ds(pl.multiple_of(half * rows, rows), rows)
        col_acc[col_at, :, at] = jnp.maximum(col_acc[col_at, :, at], col_max(values))
        return carry

    for indices, full_range, half_range in groups:
        for index in indices:
            for copy in copies(index):
                copy.wait()
        if diag and 0 in indices:
            a = row_block(0)
            for part in range(2 * rows // 256):
                values = product(a, part * 256, 256)
                offset = (
                    lax.broadcasted_iota(jnp.int32, values.shape, 1)
                    - lax.broadcasted_iota(jnp.int32, values.shape, 0)
                    + (part * 256 - core * rows)
                )
                earlier = jnp.where(offset < -exclude, values, LOW)
                later = jnp.where(offset > exclude, values, LOW)
                row_acc[0] = jnp.maximum(row_acc[0], row_max(earlier))
                row_acc[1] = jnp.maximum(row_acc[1], row_max(later))
        if full_range[1] > full_range[0]:
            lax.fori_loop(full_range[0], full_range[1], visit, 0)
        if half_range[1] > half_range[0]:
            lax.fori_loop(half_range[0], half_range[1], visit_half, 0)

    lanes = lax.broadcasted_iota(jnp.int32, (rows, 128), 1)
    gathered = jnp.full((rows, 128), LOW, jnp.float32)
    for at in range(row_acc.shape[0]):
        gathered = jnp.where(
            lanes == at, jnp.max(row_acc[at], axis=1, keepdims=True), gathered
        )
    turned = gathered.T[: out.shape[0]]
    total = jnp.max(col_acc[...], axis=1)
    if has_prev:
        total = jnp.maximum(total, prev[...])
    out[...] = total
    at = pl.ds(pl.multiple_of(core * rows, rows), rows)
    out[:, at] = jnp.maximum(out[:, at], turned)


def merge_kernel(n_moved, meta, mine_ref, other_ref, *outs):
    core = meta[0]
    best = jnp.maximum(mine_ref[...], other_ref[...])
    outs[0][...] = best[0:2]
    for i in range(n_moved):
        at = 2 + 4 * i
        outs[1 + i][...] = jnp.where(core == 0, best[at : at + 2], best[at + 2 : at + 4])


def finish_kernel(rows, meta, mine_ref, other_ref, o_ref):
    at = pl.ds(pl.multiple_of(meta[0] * rows, rows), rows)
    o_ref[...] = 1.0 - jnp.maximum(mine_ref[:, at], other_ref[:, at])


SMEM = pl.BlockSpec(memory_space=pltpu.SMEM)
VMEM = pl.BlockSpec(memory_space=pltpu.VMEM)
ANY = pl.BlockSpec(memory_space=pl.ANY)


def shards(segments, exclusion):
    rows, length = segments.shape
    n_moved = len(OFFSETS)
    device = lax.axis_index("row") * 16 + lax.axis_index("col")
    core = device % 2
    x = device // 8 % 2 * 2 + device // 16 % 2
    y = device // 32
    z = device // 2 % SIDE
    off = np.array(SLOTS, np.int32)
    sx, sy, sz = (x + off[:, 0]) % SIDE, (y + off[:, 1]) % SIDE, (z + off[:, 2]) % SIDE
    order = ((sy * 2 + sx % 2) * 2 + sx // 2) * SIDE + sz
    meta = jnp.concatenate([core[None], exclusion, order]).astype(jnp.int32)

    own = pl.pallas_call(
        normalize_kernel, out_shape=jax.ShapeDtypeStruct((rows, length), jnp.bfloat16)
    )(segments)
    other = lax.ppermute(own, AXES, across())
    block = jnp.concatenate([own, other], axis=0)

    moved, shared = [], []
    for i, offsets in enumerate(OFFSETS):
        source = SOURCES[i]
        if source is None:
            moved.append(lax.ppermute(block, AXES, moves(offsets)))
        else:
            hops = tuple(minus(a, b) for a, b in zip(offsets, OFFSETS[source]))
            moved.append(lax.ppermute(moved[source], AXES, moves(hops)))
    for i in range(n_moved):
        shared.append(lax.ppermute(moved[i], AXES, across()))

    full, half = pair_lists()

    def phase(count, pairs, halves, groups, diag, prev):
        n_acc = 2 * len(SLOTS)
        table = np.array(pairs + halves, np.int32).reshape(-1)
        operands = [meta, jnp.asarray(table), block]
        for i in range(count):
            operands += [moved[i], shared[i]]
        specs = [SMEM, SMEM] + [ANY] * (1 + 2 * count)
        if prev is not None:
            operands.append(prev)
            specs.append(VMEM)
        n_products = len(pairs) + len(halves) / 2 + diag
        return pl.pallas_call(
            functools.partial(phase_kernel, count, groups, diag, prev is not None, rows),
            out_shape=jax.ShapeDtypeStruct((n_acc, 2 * rows), jnp.float32),
            in_specs=specs,
            out_specs=VMEM,
            scratch_shapes=[
                pltpu.VMEM(((1 + 2 * count) * 2 * rows, length), jnp.bfloat16),
                pltpu.VMEM((n_acc, rows, 128), jnp.float32),
                pltpu.VMEM((n_acc, 8, 2 * rows), jnp.float32),
                pltpu.SemaphoreType.DMA((1 + 2 * count, 2)),
            ],
            compiler_params=pltpu.CompilerParams(vmem_limit_bytes=48 * 2**20),
            cost_estimate=pl.CostEstimate(
                flops=int(4 * n_products * rows * rows * length),
                bytes_accessed=(1 + 2 * count) * 4 * rows * length,
                transcendentals=0,
            ),
        )(*operands)

    def stage(pair):
        return (max(pair) + 1) // 2

    first = 3
    pairs = sorted((p for p in full if stage(p) <= first), key=stage)
    halves = sorted((p for p in half if stage(p) <= first), key=stage)
    groups, i, j = [], 0, len(pairs)
    for step in range(first + 1):
        indices = (0,) if step == 0 else (2 * step - 1, 2 * step)
        i_end = i + sum(stage(p) == step for p in pairs)
        j_end = j + sum(stage(p) == step for p in halves)
        groups.append((indices, (i, i_end), (j, j_end)))
        i, j = i_end, j_end
    best = phase(first, pairs, halves, tuple(groups), True, None)

    pairs = [p for p in full if stage(p) > first]
    halves = [p for p in half if stage(p) > first]
    groups = (
        (tuple(range(1 + 2 * n_moved)), (0, len(pairs)), (len(pairs), len(pairs) + len(halves))),
    )
    best = phase(n_moved, pairs, halves, groups, False, best)

    shape = jax.ShapeDtypeStruct((2, 2 * rows), jnp.float32)
    parts = pl.pallas_call(
        functools.partial(merge_kernel, n_moved),
        out_shape=[shape] * (1 + n_moved),
        in_specs=[SMEM, VMEM, VMEM],
        out_specs=[VMEM] * (1 + n_moved),
    )(meta, best, lax.ppermute(best, AXES, across()))
    mine = parts[0]
    for i, offsets in enumerate(OFFSETS):
        back = tuple(minus((0, 0, 0), a) for a in offsets)
        mine = jnp.maximum(mine, lax.ppermute(parts[1 + i], AXES, moves(back)))
    return pl.pallas_call(
        functools.partial(finish_kernel, rows),
        out_shape=jax.ShapeDtypeStruct((2, rows), jnp.float32),
        in_specs=[SMEM, VMEM, VMEM],
        out_specs=VMEM,
    )(meta, mine, lax.ppermute(mine, AXES, across()))


def solution(mesh):
    return jax.shard_map(
        shards,
        mesh=mesh,
        in_specs=(P(AXES, None), P()),
        out_specs=P(None, AXES),
        check_vma=False,
    )
```

```python
import functools
import itertools
import math

import jax
import jax.numpy as jnp
from jax import lax
from jax.experimental import pallas as pl
from jax.experimental.pallas import tpu as pltpu
from jax.sharding import PartitionSpec as P

AXES = ("row", "col")
SIDE = 4
HELD = (
    ((0, 0, 0), (0, 1, 0), (3, 0, 1), (0, 2, 0), (2, 0, 1), (1, 3, 3)),
    ((0, 0, 0), (1, 3, 0), (0, 0, 3), (2, 2, 0), (0, 0, 2), (1, 2, 1)),
)
SOURCE = (None, 0, 0, 1, 2, 3)
MOVED = 5
SHARED = (1, 2, 3)
FIRST = ((1, 0), (2, 0), (2, 1))
SECOND = ((1, 6), (2, 6), (2, 7))
THIRD = ((3, 0), (3, 6), (4, 0), (4, 1), (4, 2), (4, 6), (4, 7), (4, 3), (3, 8), (4, 8))
LAST = ((5, 0), (5, 1), (5, 2), (5, 4))
LOW = -3.0


def minus(a, b):
    return tuple((p - q) % SIDE for p, q in zip(a, b))


def coords(device):
    row, col = divmod(device, 16)
    y, x_lo = divmod(row, 2)
    return (col // 8 * 2 + x_lo, y, col // 2 % SIDE, col % 2)


def device_at(x, y, z, core):
    x, y, z = x % SIDE, y % SIDE, z % SIDE
    return (y * 2 + x % 2) * 16 + x // 2 * 8 + z * 2 + core


def moves(hops):
    out = []
    for target in range(128):
        x, y, z, core = coords(target)
        dx, dy, dz = hops[core]
        out.append((device_at(x + dx, y + dy, z + dz, core), target))
    return out


def across():
    return [(device, device ^ 1) for device in range(128)]


def offset_of(name, core):
    return HELD[core][name] if name <= MOVED else HELD[1 - core][name - MOVED]


def check_cover():
    seen = {(0, 0, 0)}
    for a, b in FIRST + SECOND + THIRD + LAST:
        for core in (0, 1):
            diff = minus(offset_of(a, core), offset_of(b, core))
            seen |= {diff, minus((0, 0, 0), diff)}
    assert seen == set(itertools.product(range(SIDE), repeat=3))


def may_touch(a, b):
    steps = {(0, 0, 1), (2, 0, 1), (3, 0, 1), (1, 1, 1)}
    steps |= {minus((0, 0, 0), step) for step in steps}
    return any(minus(offset_of(a, core), offset_of(b, core)) in steps for core in (0, 1))


def normalize_kernel(own_ref, other_ref, o_ref):
    rows, length = own_ref.shape
    for at, ref in ((0, own_ref), (rows, other_ref)):
        x = ref[...]
        average = jnp.sum(x, axis=1, keepdims=True) * (1.0 / length)
        centered = x - average
        power = jnp.sum(centered * centered, axis=1, keepdims=True) * (1.0 / length)
        spread_inv = lax.rsqrt(power + 1e-05) * (1.0 / math.sqrt(length))
        o_ref[at : at + rows] = (centered * spread_inv).astype(jnp.bfloat16)


def here():
    row, col = lax.axis_index("row"), lax.axis_index("col")
    x = (col >> 3) * 2 + (row & 1)
    return x, row >> 1, (col >> 1) & 3, col & 1


def order_of(name, place):
    x, y, z, core = place
    zero, one = offset_of(name, 0), offset_of(name, 1)
    sx, sy, sz = (
        (p + (a if a == b else jnp.where(core == 0, a, b))) & 3
        for p, a, b in zip((x, y, z), zero, one)
    )
    order = ((sy * 2 + (sx & 1)) * 2 + (sx >> 1)) * SIDE + sz
    return order, core if name <= MOVED else 1 - core


def positions(shape, dim, first, order, flip, size):
    at = lax.broadcasted_iota(jnp.int32, shape, dim) + (first + flip * (size // 2))
    return order * size + jnp.where(at >= size, at - size, at)


def phase_kernel(names, pairs, diag, n_prev, n_out, *refs):
    exclude_ref = refs[0]
    blocks = dict(zip(names, refs[1 : 1 + len(names)]))
    rest = refs[1 + len(names) :]
    prev, rest = rest[:n_prev], rest[n_prev:]
    outs, (row_acc, col_acc) = rest[:-2], rest[-2:]
    exclude = exclude_ref[0]
    place = here()
    size = blocks[names[0]].shape[0]
    width = 256
    row_names = sorted({a for a, _ in pairs} | ({0} if diag else set()))
    col_names = sorted({b for _, b in pairs})

    row_acc[...] = jnp.full(row_acc.shape, LOW, jnp.float32)
    col_acc[...] = jnp.full(col_acc.shape, LOW, jnp.float32)

    def product(a, b, part):
        return lax.dot_general(
            blocks[a][...],
            blocks[b][part * width : (part + 1) * width],
            (((1,), (1,)), ((), ())),
            preferred_element_type=jnp.float32,
        )

    def row_max(values):
        best = values[:, :128]
        for at in range(128, width, 128):
            best = jnp.maximum(best, values[:, at : at + 128])
        return best

    def col_max(values):
        return jnp.max(values.reshape(size // 8, 8, width), axis=0)

    def apart(a, b, part):
        order_a, flip_a = order_of(a, place)
        order_b, flip_b = order_of(b, place)
        shape = (size, width)
        return positions(shape, 1, part * width, order_b, flip_b, size) - positions(
            shape, 0, 0, order_a, flip_a, size
        )

    def visit(a, b, masked):
        later = (order_of(b, place)[0] > order_of(a, place)[0]).astype(jnp.int32)
        row_at = 2 * row_names.index(a) + later
        col_at = 2 * col_names.index(b) + 1 - later
        for part in range(size // width):
            values = product(a, b, part)
            if masked:
                values = jnp.where(jnp.abs(apart(a, b, part)) > exclude, values, LOW)
            row_acc[row_at] = jnp.maximum(row_acc[row_at], row_max(values))
            at = pl.ds(part * width, width)
            col_acc[col_at, :, at] = jnp.maximum(col_acc[col_at, :, at], col_max(values))

    if diag:
        at = 2 * row_names.index(0)
        for part in range(size // width):
            values = product(0, 0, part)
            offset = apart(0, 0, part)
            earlier = jnp.where(offset < -exclude, values, LOW)
            later = jnp.where(offset > exclude, values, LOW)
            row_acc[at] = jnp.maximum(row_acc[at], row_max(earlier))
            row_acc[at + 1] = jnp.maximum(row_acc[at + 1], row_max(later))
    for a, b in pairs:
        if may_touch(a, b):
            near = jnp.abs(order_of(a, place)[0] - order_of(b, place)[0]) == 1
            pl.when(near)(functools.partial(visit, a, b, True))
            pl.when(jnp.logical_not(near))(functools.partial(visit, a, b, False))
        else:
            visit(a, b, False)

    lanes = lax.broadcasted_iota(jnp.int32, (size, 128), 1)
    gathered = jnp.full((size, 128), LOW, jnp.float32)
    for at in range(2 * len(row_names)):
        gathered = jnp.where(
            lanes == at, jnp.max(row_acc[at], axis=1, keepdims=True), gathered
        )
    turned = gathered.T
    folded = jnp.max(col_acc[...], axis=1)

    def result(name):
        parts = []
        if name in row_names:
            at = 2 * row_names.index(name)
            parts.append(turned[at : at + 2])
        if name in col_names:
            at = 2 * col_names.index(name)
            parts.append(folded[at : at + 2])
        if n_prev and (name <= MOVED or not isinstance(n_out, tuple)):
            parts.append(prev[0][2 * name : 2 * name + 2])
        elif n_prev and name > MOVED:
            parts.append(prev[1][2 * (name - MOVED - 1) : 2 * (name - MOVED)])
        if n_out == "each" and name in SHARED:
            at = 2 * SHARED.index(name)
            parts.append(prev[1][at : at + 2])
        return functools.reduce(jnp.maximum, parts) if parts else jnp.full((2, size), LOW)

    if n_out == "each":
        for name in range(MOVED + 1):
            outs[name][...] = result(name)
    else:
        for name in range(MOVED + 1):
            outs[0][2 * name : 2 * name + 2] = result(name)
        for i, name in enumerate(SHARED):
            outs[1][2 * i : 2 * i + 2] = result(MOVED + name)


SMEM = pl.BlockSpec(memory_space=pltpu.SMEM)
VMEM = pl.BlockSpec(memory_space=pltpu.VMEM)


def shards(segments, exclusion):
    check_cover()
    rows, length = segments.shape
    size = 2 * rows
    float32 = jnp.float32

    def phase(pairs, blocks, prev, diag=False, each=False):
        names = sorted({name for pair in pairs for name in pair} | ({0} if diag else set()))
        rows_of = {a for a, _ in pairs} | ({0} if diag else set())
        cols_of = {b for _, b in pairs}
        if each:
            out_shape = [jax.ShapeDtypeStruct((2, size), float32)] * (MOVED + 1)
        else:
            out_shape = [
                jax.ShapeDtypeStruct((2 * MOVED + 2, size), float32),
                jax.ShapeDtypeStruct((2 * len(SHARED), size), float32),
            ]
        count = len(pairs) + diag
        return pl.pallas_call(
            functools.partial(
                phase_kernel, names, pairs, diag, len(prev), "each" if each else (2,)
            ),
            out_shape=out_shape,
            in_specs=[SMEM] + [VMEM] * (len(names) + len(prev)),
            out_specs=[VMEM] * len(out_shape),
            scratch_shapes=[
                pltpu.VMEM((2 * len(rows_of), size, 128), float32),
                pltpu.VMEM((2 * max(len(cols_of), 1), 8, size), float32),
            ],
            compiler_params=pltpu.CompilerParams(vmem_limit_bytes=40 * 2**20),
            cost_estimate=pl.CostEstimate(
                flops=2 * count * size * size * length,
                bytes_accessed=len(names) * 2 * size * length,
                transcendentals=0,
            ),
        )(exclusion, *[blocks[name] for name in names], *prev)

    block = pl.pallas_call(
        normalize_kernel, out_shape=jax.ShapeDtypeStruct((size, length), jnp.bfloat16)
    )(segments, lax.ppermute(segments, AXES, across()))

    blocks = {0: block}

    def move(i):
        hops = tuple(minus(HELD[c][i], HELD[c][SOURCE[i]]) for c in (0, 1))
        blocks[i] = lax.ppermute(blocks[SOURCE[i]], AXES, moves(hops))

    def share(i):
        blocks[MOVED + i] = lax.ppermute(blocks[i], AXES, across())

    def after(i, done):
        blocks[i], done = lax.optimization_barrier((blocks[i], done))
        return done

    move(1)
    move(2)
    best = phase((), blocks, (), diag=True)
    best = after(1, best)
    best = after(2, best)
    move(3)
    move(4)
    share(1)
    share(2)
    best = phase(FIRST, blocks, best)
    best = phase(SECOND, blocks, best)
    best = after(3, best)
    best = after(4, best)
    move(5)
    share(3)
    best = phase(THIRD, blocks, best)
    best = after(5, best)
    parts = phase(LAST, blocks, (best[0], lax.ppermute(best[1], AXES, across())), each=True)

    mine = parts[0]
    for i in range(1, MOVED + 1):
        back = tuple(minus((0, 0, 0), HELD[c][i]) for c in (0, 1))
        mine = jnp.maximum(mine, lax.ppermute(parts[i], AXES, moves(back)))
    other = lax.ppermute(mine, AXES, across())
    return 1.0 - jnp.maximum(mine[:, :rows], other[:, rows:])


def solution(mesh):
    return jax.shard_map(
        shards,
        mesh=mesh,
        in_specs=(P(AXES, None), P()),
        out_specs=P(None, AXES),
        check_vma=False,
    )
```

```python
import functools
import itertools
import math

import jax
import jax.numpy as jnp
from jax import lax
from jax.experimental import pallas as pl
from jax.experimental.pallas import tpu as pltpu
from jax.sharding import PartitionSpec as P

AXES = ("row", "col")
SIDE = 4
HELD = (
    ((0, 0, 0), (0, 1, 1), (0, 0, 3), (3, 1, 1), (0, 0, 2), (3, 1, 2)),
    ((0, 0, 0), (3, 3, 0), (1, 0, 0), (3, 2, 0), (2, 0, 0), (2, 2, 0)),
)
SOURCE = (None, 0, 0, 1, 2, 3)
MOVED = 5
SHARED = (1, 2, 3, 4)
FIRST = ((1, 0), (2, 0), (2, 1))
SECOND = ((1, 6), (2, 6), (2, 7))
THIRD = ((3, 0), (3, 1), (3, 2), (3, 6), (3, 7), (4, 0), (4, 7))
FOURTH = ((3, 8), (4, 8), (4, 9))
LAST = ((5, 1), (5, 4), (5, 6), (5, 7), (5, 9))
LOW = -3.0


def minus(a, b):
    return tuple((p - q) % SIDE for p, q in zip(a, b))


def coords(device):
    row, col = divmod(device, 16)
    y, x_lo = divmod(row, 2)
    return (col // 8 * 2 + x_lo, y, col // 2 % SIDE, col % 2)


def device_at(x, y, z, core):
    x, y, z = x % SIDE, y % SIDE, z % SIDE
    return (y * 2 + x % 2) * 16 + x // 2 * 8 + z * 2 + core


def moves(hops):
    out = []
    for target in range(128):
        x, y, z, core = coords(target)
        dx, dy, dz = hops[core]
        out.append((device_at(x + dx, y + dy, z + dz, core), target))
    return out


def across():
    return [(device, device ^ 1) for device in range(128)]


def offset_of(name, core):
    return HELD[core][name] if name <= MOVED else HELD[1 - core][name - MOVED]


def check_cover():
    seen = {(0, 0, 0)}
    for a, b in FIRST + SECOND + THIRD + FOURTH + LAST:
        for core in (0, 1):
            diff = minus(offset_of(a, core), offset_of(b, core))
            seen |= {diff, minus((0, 0, 0), diff)}
    assert seen == set(itertools.product(range(SIDE), repeat=3))


def may_touch(a, b):
    steps = {(0, 0, 1), (2, 0, 1), (3, 0, 1), (1, 1, 1)}
    steps |= {minus((0, 0, 0), step) for step in steps}
    return any(minus(offset_of(a, core), offset_of(b, core)) in steps for core in (0, 1))


def normalize(x):
    length = x.shape[1]
    average = jnp.sum(x, axis=1, keepdims=True) * (1.0 / length)
    centered = x - average
    power = jnp.sum(centered * centered, axis=1, keepdims=True) * (1.0 / length)
    spread_inv = lax.rsqrt(power + 1e-05) * (1.0 / math.sqrt(length))
    return (centered * spread_inv).astype(jnp.bfloat16)


def own_kernel(x_ref, o_ref):
    o_ref[...] = normalize(x_ref[...])


def both_kernel(own_ref, other_ref, o_ref):
    rows = own_ref.shape[0]
    o_ref[:rows] = own_ref[...]
    o_ref[rows:] = normalize(other_ref[...])


def here():
    row, col = lax.axis_index("row"), lax.axis_index("col")
    x = (col >> 3) * 2 + (row & 1)
    return x, row >> 1, (col >> 1) & 3, col & 1


def order_of(name, place):
    x, y, z, core = place
    zero, one = offset_of(name, 0), offset_of(name, 1)
    sx, sy, sz = (
        (p + (a if a == b else jnp.where(core == 0, a, b))) & 3
        for p, a, b in zip((x, y, z), zero, one)
    )
    order = ((sy * 2 + (sx & 1)) * 2 + (sx >> 1)) * SIDE + sz
    return order, core if name <= MOVED else 1 - core


def positions(shape, dim, first, order, flip, size):
    at = lax.broadcasted_iota(jnp.int32, shape, dim) + (first + flip * (size // 2))
    return order * size + jnp.where(at >= size, at - size, at)


def phase_kernel(names, pairs, diag, n_prev, each, *refs):
    exclude_ref = refs[0]
    blocks = dict(zip(names, refs[1 : 1 + len(names)]))
    rest = refs[1 + len(names) :]
    prev, rest = rest[:n_prev], rest[n_prev:]
    outs, (row_acc, col_acc) = rest[:-2], rest[-2:]
    exclude = exclude_ref[0]
    place = here()
    size = blocks[names[0]].shape[0]
    width = 256
    row_names = sorted({a for a, _ in pairs} | ({0} if diag else set()))
    col_names = sorted({b for _, b in pairs})

    row_acc[...] = jnp.full(row_acc.shape, LOW, jnp.float32)
    col_acc[...] = jnp.full(col_acc.shape, LOW, jnp.float32)

    def product(a, b, part):
        return lax.dot_general(
            blocks[a][...],
            blocks[b][part * width : (part + 1) * width],
            (((1,), (1,)), ((), ())),
            preferred_element_type=jnp.float32,
        )

    def row_max(values):
        best = values[:, :128]
        for at in range(128, width, 128):
            best = jnp.maximum(best, values[:, at : at + 128])
        return best

    def col_max(values):
        return jnp.max(values.reshape(size // 8, 8, width), axis=0)

    def apart(a, b, part):
        order_a, flip_a = order_of(a, place)
        order_b, flip_b = order_of(b, place)
        shape = (size, width)
        return positions(shape, 1, part * width, order_b, flip_b, size) - positions(
            shape, 0, 0, order_a, flip_a, size
        )

    def visit(a, b, masked):
        later = (order_of(b, place)[0] > order_of(a, place)[0]).astype(jnp.int32)
        row_at = 2 * row_names.index(a) + later
        col_at = 2 * col_names.index(b) + 1 - later
        for part in range(size // width):
            values = product(a, b, part)
            if masked:
                values = jnp.where(jnp.abs(apart(a, b, part)) > exclude, values, LOW)
            row_acc[row_at] = jnp.maximum(row_acc[row_at], row_max(values))
            at = pl.ds(part * width, width)
            col_acc[col_at, :, at] = jnp.maximum(col_acc[col_at, :, at], col_max(values))

    if diag:
        at = 2 * row_names.index(0)
        for part in range(size // width):
            values = product(0, 0, part)
            offset = apart(0, 0, part)
            earlier = jnp.where(offset < -exclude, values, LOW)
            later = jnp.where(offset > exclude, values, LOW)
            row_acc[at] = jnp.maximum(row_acc[at], row_max(earlier))
            row_acc[at + 1] = jnp.maximum(row_acc[at + 1], row_max(later))
    for a, b in pairs:
        if may_touch(a, b):
            near = jnp.abs(order_of(a, place)[0] - order_of(b, place)[0]) == 1
            pl.when(near)(functools.partial(visit, a, b, True))
            pl.when(jnp.logical_not(near))(functools.partial(visit, a, b, False))
        else:
            visit(a, b, False)

    lanes = lax.broadcasted_iota(jnp.int32, (size, 128), 1)
    gathered = jnp.full((size, 128), LOW, jnp.float32)
    for at in range(2 * len(row_names)):
        gathered = jnp.where(
            lanes == at, jnp.max(row_acc[at], axis=1, keepdims=True), gathered
        )
    turned = gathered.T
    folded = jnp.max(col_acc[...], axis=1)

    def result(name):
        parts = []
        if name in row_names:
            at = 2 * row_names.index(name)
            parts.append(turned[at : at + 2])
        if name in col_names:
            at = 2 * col_names.index(name)
            parts.append(folded[at : at + 2])
        if n_prev and name <= MOVED:
            parts.append(prev[0][2 * name : 2 * name + 2])
        elif n_prev:
            at = 2 * SHARED.index(name - MOVED)
            parts.append(prev[1][at : at + 2])
        return functools.reduce(jnp.maximum, parts) if parts else jnp.full((2, size), LOW)

    for name in range(MOVED + 1):
        if each:
            outs[name][...] = result(name)
        else:
            outs[0][2 * name : 2 * name + 2] = result(name)
    for i, name in enumerate(SHARED):
        outs[-1][2 * i : 2 * i + 2] = result(MOVED + name)


def merge_kernel(*refs):
    mine, other, outs = refs[: len(SHARED)], refs[len(SHARED)], refs[len(SHARED) + 1 :]
    for i in range(len(SHARED)):
        outs[i][...] = jnp.maximum(mine[i][...], other[2 * i : 2 * i + 2])


SMEM = pl.BlockSpec(memory_space=pltpu.SMEM)
VMEM = pl.BlockSpec(memory_space=pltpu.VMEM)


def shards(segments, exclusion):
    check_cover()
    rows, length = segments.shape
    size = 2 * rows
    float32 = jnp.float32

    def phase(pairs, blocks, prev, diag=False, each=False):
        names = sorted({name for pair in pairs for name in pair} | ({0} if diag else set()))
        rows_of = {a for a, _ in pairs} | ({0} if diag else set())
        cols_of = {b for _, b in pairs}
        part = jax.ShapeDtypeStruct((2, size), float32)
        own_part = jax.ShapeDtypeStruct((2 * MOVED + 2, size), float32)
        out_shape = [part] * (MOVED + 1) if each else [own_part]
        out_shape.append(jax.ShapeDtypeStruct((2 * len(SHARED), size), float32))
        count = len(pairs) + diag
        return pl.pallas_call(
            functools.partial(
                phase_kernel, names, pairs, diag, len(prev), each
            ),
            out_shape=out_shape,
            in_specs=[SMEM] + [VMEM] * (len(names) + len(prev)),
            out_specs=[VMEM] * len(out_shape),
            scratch_shapes=[
                pltpu.VMEM((2 * len(rows_of), size, 128), float32),
                pltpu.VMEM((2 * max(len(cols_of), 1), 8, size), float32),
            ],
            compiler_params=pltpu.CompilerParams(vmem_limit_bytes=20 * 2**20),
            cost_estimate=pl.CostEstimate(
                flops=8 * 2 * count * size * size * length,
                bytes_accessed=2 * size * len(names),
                transcendentals=0,
            ),
        )(exclusion, *[blocks[name] for name in names], *prev)

    other = lax.ppermute(segments, AXES, across())
    own = pl.pallas_call(
        own_kernel,
        out_shape=jax.ShapeDtypeStruct((rows, length), jnp.bfloat16),
        in_specs=[VMEM],
        out_specs=VMEM,
        compiler_params=pltpu.CompilerParams(vmem_limit_bytes=8 * 2**20),
    )(segments)
    block = pl.pallas_call(
        both_kernel,
        out_shape=jax.ShapeDtypeStruct((size, length), jnp.bfloat16),
        in_specs=[VMEM, VMEM],
        out_specs=VMEM,
        compiler_params=pltpu.CompilerParams(vmem_limit_bytes=8 * 2**20),
    )(own, other)

    blocks = {0: block}

    def move(i):
        hops = tuple(minus(HELD[c][i], HELD[c][SOURCE[i]]) for c in (0, 1))
        blocks[i] = lax.ppermute(blocks[SOURCE[i]], AXES, moves(hops))

    def share(i):
        blocks[MOVED + i] = lax.ppermute(blocks[i], AXES, across())

    def after(i, done):
        blocks[i], done = lax.optimization_barrier((blocks[i], done))
        return done

    move(1)
    move(2)
    move(3)
    move(4)
    share(1)
    share(2)
    best = phase(FIRST, blocks, (), diag=True)
    best = phase(SECOND, blocks, best)
    best = after(3, best)
    move(5)
    share(3)
    share(4)
    best = phase(THIRD, blocks, best)
    best = phase(FOURTH, blocks, best)
    best = after(5, best)
    *parts, lent = phase(LAST, blocks, best, each=True)

    def give(i, part):
        back = tuple(minus((0, 0, 0), HELD[c][i]) for c in (0, 1))
        return lax.ppermute(part, AXES, moves(back))

    lent = lax.ppermute(lent, AXES, across())
    mine = jnp.maximum(parts[0], give(5, parts[5]))
    merged = pl.pallas_call(
        merge_kernel,
        out_shape=[jax.ShapeDtypeStruct((2, size), float32)] * len(SHARED),
        in_specs=[VMEM] * (len(SHARED) + 1),
        out_specs=[VMEM] * len(SHARED),
        compiler_params=pltpu.CompilerParams(vmem_limit_bytes=4 * 2**20),
    )(*[parts[i] for i in SHARED], lent)
    for i in (4, 3, 2, 1):
        mine = jnp.maximum(mine, give(i, merged[i - 1]))
    other = lax.ppermute(mine, AXES, across())
    return 1.0 - jnp.maximum(mine[:, :rows], other[:, rows:])


def solution(mesh):
    return jax.shard_map(
        shards,
        mesh=mesh,
        in_specs=(P(AXES, None), P()),
        out_specs=P(None, AXES),
        check_vma=False,
    )
```

```python
import functools
import itertools
import math

import jax
import jax.numpy as jnp
from jax import lax
from jax.experimental import pallas as pl
from jax.experimental.pallas import tpu as pltpu
from jax.sharding import PartitionSpec as P

AXES = ("row", "col")
SIDE = 4
HELD = (
    ((0, 0, 0), (0, 1, 1), (0, 0, 3), (3, 1, 1), (0, 0, 2), (3, 1, 2)),
    ((0, 0, 0), (3, 3, 0), (1, 0, 0), (3, 2, 0), (2, 0, 0), (2, 2, 0)),
)
SOURCE = (None, 0, 0, 1, 2, 3)
MOVED = 5
HALVED = (1, 3, 5)
SHARED = (1, 2, 3, 4)
FIRST = ((1, 0), (2, 0), (2, 1))
SECOND = ((1, 6), (2, 6), (2, 7))
THIRD = ((3, 0), (3, 1), (3, 2), (3, 6), (3, 7), (4, 0), (4, 7))
FOURTH = ((3, 8), (4, 8), (4, 9))
LAST = ((5, 1), (5, 4), (5, 6), (5, 7), (5, 9))
LOW = -3.0


def minus(a, b):
    return tuple((p - q) % SIDE for p, q in zip(a, b))


def coords(device):
    row, col = divmod(device, 16)
    y, x_lo = divmod(row, 2)
    return (col // 8 * 2 + x_lo, y, col // 2 % SIDE, col % 2)


def device_at(x, y, z, core):
    x, y, z = x % SIDE, y % SIDE, z % SIDE
    return (y * 2 + x % 2) * 16 + x // 2 * 8 + z * 2 + core


def moves(hops):
    out = []
    for target in range(128):
        x, y, z, core = coords(target)
        dx, dy, dz = hops[core]
        out.append((device_at(x + dx, y + dy, z + dz, core), target))
    return out


def across():
    return [(device, device ^ 1) for device in range(128)]


def offset_of(name, core):
    return HELD[core][name] if name <= MOVED else HELD[1 - core][name - MOVED]


def check_cover():
    seen = {(0, 0, 0)}
    for a, b in FIRST + SECOND + THIRD + FOURTH + LAST:
        for core in (0, 1):
            diff = minus(offset_of(a, core), offset_of(b, core))
            seen |= {diff, minus((0, 0, 0), diff)}
    assert seen == set(itertools.product(range(SIDE), repeat=3))


def may_touch(a, b):
    steps = {(0, 0, 1), (2, 0, 1), (3, 0, 1), (1, 1, 1)}
    steps |= {minus((0, 0, 0), step) for step in steps}
    return any(minus(offset_of(a, core), offset_of(b, core)) in steps for core in (0, 1))


def normalize(x):
    length = x.shape[1]
    average = jnp.sum(x, axis=1, keepdims=True) * (1.0 / length)
    centered = x - average
    power = jnp.sum(centered * centered, axis=1, keepdims=True) * (1.0 / length)
    spread_inv = lax.rsqrt(power + 1e-05) * (1.0 / math.sqrt(length))
    return (centered * spread_inv).astype(jnp.bfloat16)


def own_kernel(x_ref, o_ref):
    o_ref[...] = normalize(x_ref[...])


def both_kernel(own_ref, other_ref, half_ref, o_ref):
    rows = own_ref.shape[0]
    half = normalize(other_ref[...])
    half_ref[...] = half
    o_ref[:rows] = own_ref[...]
    o_ref[rows:] = half


def here():
    row, col = lax.axis_index("row"), lax.axis_index("col")
    x = (col >> 3) * 2 + (row & 1)
    return x, row >> 1, (col >> 1) & 3, col & 1


def order_of(name, place):
    x, y, z, core = place
    zero, one = offset_of(name, 0), offset_of(name, 1)
    sx, sy, sz = (
        (p + (a if a == b else jnp.where(core == 0, a, b))) & 3
        for p, a, b in zip((x, y, z), zero, one)
    )
    order = ((sy * 2 + (sx & 1)) * 2 + (sx >> 1)) * SIDE + sz
    return order, core if name <= MOVED else 1 - core


def positions(shape, dim, first, order, flip, size):
    at = lax.broadcasted_iota(jnp.int32, shape, dim) + (first + flip * (size // 2))
    return order * size + jnp.where(at >= size, at - size, at)


def phase_kernel(names, counts, pairs, diag, n_prev, each, *refs):
    exclude_ref = refs[0]
    rest = refs[1:]
    pieces = {}
    for name, count in zip(names, counts):
        pieces[name], rest = rest[:count], rest[count:]
    prev, rest = rest[:n_prev], rest[n_prev:]
    outs, (whole, row_acc, col_acc) = rest[:-3], rest[-3:]
    exclude = exclude_ref[0]
    place = here()
    size = whole.shape[1]
    blocks = {}
    for name, parts in pieces.items():
        if len(parts) == 1:
            blocks[name] = parts[0]
        else:
            blocks[name] = whole.at[sum(len(pieces[other]) > 1 for other in names if other < name)]
            for i, part in enumerate(parts):
                blocks[name][i * part.shape[0] : (i + 1) * part.shape[0]] = part[...]
    width = 256
    row_names = sorted({a for a, _ in pairs} | ({0} if diag else set()))
    col_names = sorted({b for _, b in pairs})

    row_acc[...] = jnp.full(row_acc.shape, LOW, jnp.float32)
    col_acc[...] = jnp.full(col_acc.shape, LOW, jnp.float32)

    def product(a, b, part):
        return lax.dot_general(
            blocks[a][...],
            blocks[b][part * width : (part + 1) * width],
            (((1,), (1,)), ((), ())),
            preferred_element_type=jnp.float32,
        )

    def row_max(values):
        best = values[:, :128]
        for at in range(128, width, 128):
            best = jnp.maximum(best, values[:, at : at + 128])
        return best

    def col_max(values):
        return jnp.max(values.reshape(size // 8, 8, width), axis=0)

    def apart(a, b, part):
        order_a, flip_a = order_of(a, place)
        order_b, flip_b = order_of(b, place)
        shape = (size, width)
        return positions(shape, 1, part * width, order_b, flip_b, size) - positions(
            shape, 0, 0, order_a, flip_a, size
        )

    def visit(a, b, masked):
        later = (order_of(b, place)[0] > order_of(a, place)[0]).astype(jnp.int32)
        row_at = 2 * row_names.index(a) + later
        col_at = 2 * col_names.index(b) + 1 - later
        for part in range(size // width):
            values = product(a, b, part)
            if masked:
                values = jnp.where(jnp.abs(apart(a, b, part)) > exclude, values, LOW)
            row_acc[row_at] = jnp.maximum(row_acc[row_at], row_max(values))
            at = pl.ds(part * width, width)
            col_acc[col_at, :, at] = jnp.maximum(col_acc[col_at, :, at], col_max(values))

    if diag:
        at = 2 * row_names.index(0)
        for part in range(size // width):
            values = product(0, 0, part)
            offset = apart(0, 0, part)
            earlier = jnp.where(offset < -exclude, values, LOW)
            later = jnp.where(offset > exclude, values, LOW)
            row_acc[at] = jnp.maximum(row_acc[at], row_max(earlier))
            row_acc[at + 1] = jnp.maximum(row_acc[at + 1], row_max(later))
    for a, b in pairs:
        if may_touch(a, b):
            near = jnp.abs(order_of(a, place)[0] - order_of(b, place)[0]) == 1
            pl.when(near)(functools.partial(visit, a, b, True))
            pl.when(jnp.logical_not(near))(functools.partial(visit, a, b, False))
        else:
            visit(a, b, False)

    lanes = lax.broadcasted_iota(jnp.int32, (size, 128), 1)
    gathered = jnp.full((size, 128), LOW, jnp.float32)
    for at in range(2 * len(row_names)):
        gathered = jnp.where(
            lanes == at, jnp.max(row_acc[at], axis=1, keepdims=True), gathered
        )
    turned = gathered.T
    folded = jnp.max(col_acc[...], axis=1)

    def result(name):
        parts = []
        if name in row_names:
            at = 2 * row_names.index(name)
            parts.append(turned[at : at + 2])
        if name in col_names:
            at = 2 * col_names.index(name)
            parts.append(folded[at : at + 2])
        if n_prev and name <= MOVED:
            parts.append(prev[0][2 * name : 2 * name + 2])
        elif n_prev:
            at = 2 * SHARED.index(name - MOVED)
            parts.append(prev[1][at : at + 2])
        return functools.reduce(jnp.maximum, parts) if parts else jnp.full((2, size), LOW)

    for name in range(MOVED + 1):
        if each:
            outs[name][...] = result(name)
        else:
            outs[0][2 * name : 2 * name + 2] = result(name)
    for i, name in enumerate(SHARED):
        outs[-1][2 * i : 2 * i + 2] = result(MOVED + name)


def merge_kernel(*refs):
    mine, other, outs = refs[: len(SHARED)], refs[len(SHARED)], refs[len(SHARED) + 1 :]
    for i in range(len(SHARED)):
        outs[i][...] = jnp.maximum(mine[i][...], other[2 * i : 2 * i + 2])


SMEM = pl.BlockSpec(memory_space=pltpu.SMEM)
VMEM = pl.BlockSpec(memory_space=pltpu.VMEM)


def shards(segments, exclusion):
    check_cover()
    rows, length = segments.shape
    size = 2 * rows
    float32 = jnp.float32

    def phase(pairs, blocks, prev, weight, diag=False, each=False):
        names = sorted({name for pair in pairs for name in pair} | ({0} if diag else set()))
        rows_of = {a for a, _ in pairs} | ({0} if diag else set())
        cols_of = {b for _, b in pairs}
        part = jax.ShapeDtypeStruct((2, size), float32)
        own_part = jax.ShapeDtypeStruct((2 * MOVED + 2, size), float32)
        out_shape = [part] * (MOVED + 1) if each else [own_part]
        out_shape.append(jax.ShapeDtypeStruct((2 * len(SHARED), size), float32))
        count = len(pairs) + diag
        counts = [len(blocks[name]) for name in names]
        return pl.pallas_call(
            functools.partial(
                phase_kernel, names, counts, pairs, diag, len(prev), each
            ),
            out_shape=out_shape,
            in_specs=[SMEM] + [VMEM] * (sum(counts) + len(prev)),
            out_specs=[VMEM] * len(out_shape),
            scratch_shapes=[
                pltpu.VMEM((max(1, sum(n > 1 for n in counts)), size, length), jnp.bfloat16),
                pltpu.VMEM((2 * len(rows_of), size, 128), float32),
                pltpu.VMEM((2 * max(len(cols_of), 1), 8, size), float32),
            ],
            compiler_params=pltpu.CompilerParams(vmem_limit_bytes=20 * 2**20),
            cost_estimate=pl.CostEstimate(
                flops=weight * 2 * count * size * size * length,
                bytes_accessed=2 * size * len(names),
                transcendentals=0,
            ),
        )(exclusion, *[part for name in names for part in blocks[name]], *prev)

    other = lax.ppermute(segments, AXES, across())
    own = pl.pallas_call(
        own_kernel,
        out_shape=jax.ShapeDtypeStruct((rows, length), jnp.bfloat16),
        in_specs=[VMEM],
        out_specs=VMEM,
        compiler_params=pltpu.CompilerParams(vmem_limit_bytes=8 * 2**20),
    )(segments)
    half, block = pl.pallas_call(
        both_kernel,
        out_shape=[
            jax.ShapeDtypeStruct((rows, length), jnp.bfloat16),
            jax.ShapeDtypeStruct((size, length), jnp.bfloat16),
        ],
        in_specs=[VMEM, VMEM],
        out_specs=[VMEM, VMEM],
        compiler_params=pltpu.CompilerParams(vmem_limit_bytes=8 * 2**20),
    )(own, other)

    blocks = {0: [block]}
    sources = {0: [own, half]}

    def move(i):
        hops = tuple(minus(HELD[c][i], HELD[c][SOURCE[i]]) for c in (0, 1))
        parts = sources.get(SOURCE[i], blocks[SOURCE[i]]) if i in HALVED else blocks[SOURCE[i]]
        blocks[i] = [lax.ppermute(part, AXES, moves(hops)) for part in parts]

    def share(i):
        blocks[MOVED + i] = [lax.ppermute(part, AXES, across()) for part in blocks[i]]

    def after(i, done):
        first, *rest = blocks[i]
        first, done = lax.optimization_barrier((first, done))
        blocks[i] = [first, *rest]
        return done

    move(1)
    move(2)
    best = phase((), blocks, (), 8, diag=True)
    best = after(1, best)
    move(3)
    move(4)
    share(1)
    share(2)
    best = phase(FIRST, blocks, best, 8)
    best = phase(SECOND, blocks, best, 0)
    best = after(3, best)
    move(5)
    share(3)
    share(4)
    best = phase(THIRD, blocks, best, 8)
    best = phase(FOURTH, blocks, best, 8)
    best = after(5, best)
    *parts, lent = phase(LAST, blocks, best, 1, each=True)

    def give(i, part):
        back = tuple(minus((0, 0, 0), HELD[c][i]) for c in (0, 1))
        return lax.ppermute(part, AXES, moves(back))

    lent = lax.ppermute(lent, AXES, across())
    mine = jnp.maximum(parts[0], give(5, parts[5]))
    merged = pl.pallas_call(
        merge_kernel,
        out_shape=[jax.ShapeDtypeStruct((2, size), float32)] * len(SHARED),
        in_specs=[VMEM] * (len(SHARED) + 1),
        out_specs=[VMEM] * len(SHARED),
        compiler_params=pltpu.CompilerParams(vmem_limit_bytes=4 * 2**20),
    )(*[parts[i] for i in SHARED], lent)
    for i in (4, 3, 2, 1):
        mine = jnp.maximum(mine, give(i, merged[i - 1]))
    other = lax.ppermute(mine, AXES, across())
    return 1.0 - jnp.maximum(mine[:, :rows], other[:, rows:])


def solution(mesh):
    return jax.shard_map(
        shards,
        mesh=mesh,
        in_specs=(P(AXES, None), P()),
        out_specs=P(None, AXES),
        check_vma=False,
    )
```

```python
import functools
import itertools
import math

import jax
import jax.numpy as jnp
from jax import lax
from jax.experimental import pallas as pl
from jax.experimental.pallas import tpu as pltpu
from jax.sharding import PartitionSpec as P

AXES = ("row", "col")
SIDE = 4
HELD = (
    ((0, 0, 0), (0, 1, 1), (0, 0, 3), (3, 1, 1), (0, 0, 2), (3, 1, 2)),
    ((0, 0, 0), (3, 3, 0), (1, 0, 0), (3, 2, 0), (2, 0, 0), (2, 2, 0)),
)
SOURCE = (None, 0, 0, 1, 2, 3)
MOVED = 5
HALVED = (1, 3, 5)
SHARED = (1, 2, 3, 4)
FIRST = ((1, 0), (2, 0), (2, 1))
SECOND = ((1, 6), (2, 6), (2, 7))
THIRD = ((3, 0), (3, 1), (3, 2), (3, 6), (3, 7), (4, 0), (4, 7))
LAST = ((3, 8), (4, 8), (4, 9), (5, 1), (5, 4), (5, 6), (5, 7), (5, 9))
LOW = -3.0


def minus(a, b):
    return tuple((p - q) % SIDE for p, q in zip(a, b))


def coords(device):
    row, col = divmod(device, 16)
    y, x_lo = divmod(row, 2)
    return (col // 8 * 2 + x_lo, y, col // 2 % SIDE, col % 2)


def device_at(x, y, z, core):
    x, y, z = x % SIDE, y % SIDE, z % SIDE
    return (y * 2 + x % 2) * 16 + x // 2 * 8 + z * 2 + core


def moves(hops):
    out = []
    for target in range(128):
        x, y, z, core = coords(target)
        dx, dy, dz = hops[core]
        out.append((device_at(x + dx, y + dy, z + dz, core), target))
    return out


def across():
    return [(device, device ^ 1) for device in range(128)]


def offset_of(name, core):
    return HELD[core][name] if name <= MOVED else HELD[1 - core][name - MOVED]


def check_cover():
    seen = {(0, 0, 0)}
    for a, b in FIRST + SECOND + THIRD + LAST:
        for core in (0, 1):
            diff = minus(offset_of(a, core), offset_of(b, core))
            seen |= {diff, minus((0, 0, 0), diff)}
    assert seen == set(itertools.product(range(SIDE), repeat=3))


def may_touch(a, b):
    steps = {(0, 0, 1), (2, 0, 1), (3, 0, 1), (1, 1, 1)}
    steps |= {minus((0, 0, 0), step) for step in steps}
    return any(minus(offset_of(a, core), offset_of(b, core)) in steps for core in (0, 1))


def normalize(x):
    length = x.shape[1]
    average = jnp.sum(x, axis=1, keepdims=True) * (1.0 / length)
    centered = x - average
    power = jnp.sum(centered * centered, axis=1, keepdims=True) * (1.0 / length)
    spread_inv = lax.rsqrt(power + 1e-05) * (1.0 / math.sqrt(length))
    return (centered * spread_inv).astype(jnp.bfloat16)


def own_kernel(x_ref, o_ref):
    o_ref[...] = normalize(x_ref[...])


def both_kernel(own_ref, other_ref, half_ref, o_ref):
    rows = own_ref.shape[0]
    half = normalize(other_ref[...])
    half_ref[...] = half
    o_ref[:rows] = own_ref[...]
    o_ref[rows:] = half


def here():
    row, col = lax.axis_index("row"), lax.axis_index("col")
    x = (col >> 3) * 2 + (row & 1)
    return x, row >> 1, (col >> 1) & 3, col & 1


def order_of(name, place):
    x, y, z, core = place
    zero, one = offset_of(name, 0), offset_of(name, 1)
    sx, sy, sz = (
        (p + (a if a == b else jnp.where(core == 0, a, b))) & 3
        for p, a, b in zip((x, y, z), zero, one)
    )
    order = ((sy * 2 + (sx & 1)) * 2 + (sx >> 1)) * SIDE + sz
    return order, core if name <= MOVED else 1 - core


def positions(shape, dim, first, order, flip, size):
    at = lax.broadcasted_iota(jnp.int32, shape, dim) + (first + flip * (size // 2))
    return order * size + jnp.where(at >= size, at - size, at)


def phase_kernel(names, counts, pairs, diag, n_prev, each, *refs):
    exclude_ref = refs[0]
    rest = refs[1:]
    pieces = {}
    for name, count in zip(names, counts):
        pieces[name], rest = rest[:count], rest[count:]
    prev, rest = rest[:n_prev], rest[n_prev:]
    outs, (whole, row_acc, col_acc) = rest[:-3], rest[-3:]
    exclude = exclude_ref[0]
    place = here()
    size = whole.shape[1]
    blocks = {}
    for name, parts in pieces.items():
        if len(parts) == 1:
            blocks[name] = parts[0]
        else:
            blocks[name] = whole.at[sum(len(pieces[other]) > 1 for other in names if other < name)]
            for i, part in enumerate(parts):
                blocks[name][i * part.shape[0] : (i + 1) * part.shape[0]] = part[...]
    width = 256
    row_names = sorted({a for a, _ in pairs} | ({0} if diag else set()))
    col_names = sorted({b for _, b in pairs})

    row_acc[...] = jnp.full(row_acc.shape, LOW, jnp.float32)
    col_acc[...] = jnp.full(col_acc.shape, LOW, jnp.float32)

    def product(a, b, part):
        return lax.dot_general(
            blocks[a][...],
            blocks[b][part * width : (part + 1) * width],
            (((1,), (1,)), ((), ())),
            preferred_element_type=jnp.float32,
        )

    def row_max(values):
        best = values[:, :128]
        for at in range(128, width, 128):
            best = jnp.maximum(best, values[:, at : at + 128])
        return best

    def col_max(values):
        return jnp.max(values.reshape(size // 8, 8, width), axis=0)

    def apart(a, b, part):
        order_a, flip_a = order_of(a, place)
        order_b, flip_b = order_of(b, place)
        shape = (size, width)
        return positions(shape, 1, part * width, order_b, flip_b, size) - positions(
            shape, 0, 0, order_a, flip_a, size
        )

    def visit(a, b, masked):
        later = (order_of(b, place)[0] > order_of(a, place)[0]).astype(jnp.int32)
        row_at = 2 * row_names.index(a) + later
        col_at = 2 * col_names.index(b) + 1 - later
        for part in range(size // width):
            values = product(a, b, part)
            if masked:
                values = jnp.where(jnp.abs(apart(a, b, part)) > exclude, values, LOW)
            row_acc[row_at] = jnp.maximum(row_acc[row_at], row_max(values))
            at = pl.ds(part * width, width)
            col_acc[col_at, :, at] = jnp.maximum(col_acc[col_at, :, at], col_max(values))

    if diag:
        at = 2 * row_names.index(0)
        for part in range(size // width):
            values = product(0, 0, part)
            offset = apart(0, 0, part)
            earlier = jnp.where(offset < -exclude, values, LOW)
            later = jnp.where(offset > exclude, values, LOW)
            row_acc[at] = jnp.maximum(row_acc[at], row_max(earlier))
            row_acc[at + 1] = jnp.maximum(row_acc[at + 1], row_max(later))
    for a, b in pairs:
        if may_touch(a, b):
            near = jnp.abs(order_of(a, place)[0] - order_of(b, place)[0]) == 1
            pl.when(near)(functools.partial(visit, a, b, True))
            pl.when(jnp.logical_not(near))(functools.partial(visit, a, b, False))
        else:
            visit(a, b, False)

    lanes = lax.broadcasted_iota(jnp.int32, (size, 128), 1)
    gathered = jnp.full((size, 128), LOW, jnp.float32)
    for at in range(2 * len(row_names)):
        gathered = jnp.where(
            lanes == at, jnp.max(row_acc[at], axis=1, keepdims=True), gathered
        )
    turned = gathered.T
    folded = jnp.max(col_acc[...], axis=1)

    def result(name):
        parts = []
        if name in row_names:
            at = 2 * row_names.index(name)
            parts.append(turned[at : at + 2])
        if name in col_names:
            at = 2 * col_names.index(name)
            parts.append(folded[at : at + 2])
        if n_prev and name <= MOVED:
            parts.append(prev[0][2 * name : 2 * name + 2])
        elif n_prev:
            at = 2 * SHARED.index(name - MOVED)
            parts.append(prev[1][at : at + 2])
        return functools.reduce(jnp.maximum, parts) if parts else jnp.full((2, size), LOW)

    for name in range(MOVED + 1):
        if each:
            outs[name][...] = result(name)
        else:
            outs[0][2 * name : 2 * name + 2] = result(name)
    for i, name in enumerate(SHARED):
        outs[-1][2 * i : 2 * i + 2] = result(MOVED + name)


def merge_kernel(*refs):
    mine, other, outs = refs[: len(SHARED)], refs[len(SHARED)], refs[len(SHARED) + 1 :]
    for i in range(len(SHARED)):
        outs[i][...] = jnp.maximum(mine[i][...], other[2 * i : 2 * i + 2])


SMEM = pl.BlockSpec(memory_space=pltpu.SMEM)
VMEM = pl.BlockSpec(memory_space=pltpu.VMEM)


def shards(segments, exclusion):
    check_cover()
    rows, length = segments.shape
    size = 2 * rows
    float32 = jnp.float32

    def phase(pairs, blocks, prev, weight, diag=False, each=False):
        names = sorted({name for pair in pairs for name in pair} | ({0} if diag else set()))
        rows_of = {a for a, _ in pairs} | ({0} if diag else set())
        cols_of = {b for _, b in pairs}
        part = jax.ShapeDtypeStruct((2, size), float32)
        own_part = jax.ShapeDtypeStruct((2 * MOVED + 2, size), float32)
        out_shape = [part] * (MOVED + 1) if each else [own_part]
        out_shape.append(jax.ShapeDtypeStruct((2 * len(SHARED), size), float32))
        count = len(pairs) + diag
        counts = [len(blocks[name]) for name in names]
        return pl.pallas_call(
            functools.partial(
                phase_kernel, names, counts, pairs, diag, len(prev), each
            ),
            out_shape=out_shape,
            in_specs=[SMEM] + [VMEM] * (sum(counts) + len(prev)),
            out_specs=[VMEM] * len(out_shape),
            scratch_shapes=[
                pltpu.VMEM((max(1, sum(n > 1 for n in counts)), size, length), jnp.bfloat16),
                pltpu.VMEM((2 * len(rows_of), size, 128), float32),
                pltpu.VMEM((2 * max(len(cols_of), 1), 8, size), float32),
            ],
            compiler_params=pltpu.CompilerParams(vmem_limit_bytes=20 * 2**20),
            cost_estimate=pl.CostEstimate(
                flops=weight * 2 * count * size * size * length,
                bytes_accessed=2 * size * len(names),
                transcendentals=0,
            ),
        )(exclusion, *[part for name in names for part in blocks[name]], *prev)

    other = lax.ppermute(segments, AXES, across())
    own = pl.pallas_call(
        own_kernel,
        out_shape=jax.ShapeDtypeStruct((rows, length), jnp.bfloat16),
        in_specs=[VMEM],
        out_specs=VMEM,
        compiler_params=pltpu.CompilerParams(vmem_limit_bytes=8 * 2**20),
    )(segments)
    half, block = pl.pallas_call(
        both_kernel,
        out_shape=[
            jax.ShapeDtypeStruct((rows, length), jnp.bfloat16),
            jax.ShapeDtypeStruct((size, length), jnp.bfloat16),
        ],
        in_specs=[VMEM, VMEM],
        out_specs=[VMEM, VMEM],
        compiler_params=pltpu.CompilerParams(vmem_limit_bytes=8 * 2**20),
    )(own, other)

    blocks = {0: [block]}
    sources = {0: [own, half]}

    def move(i):
        hops = tuple(minus(HELD[c][i], HELD[c][SOURCE[i]]) for c in (0, 1))
        parts = sources.get(SOURCE[i], blocks[SOURCE[i]]) if i in HALVED else blocks[SOURCE[i]]
        blocks[i] = [lax.ppermute(part, AXES, moves(hops)) for part in parts]

    def share(i):
        blocks[MOVED + i] = [lax.ppermute(part, AXES, across()) for part in blocks[i]]

    def after(i, done):
        first, *rest = blocks[i]
        first, done = lax.optimization_barrier((first, done))
        blocks[i] = [first, *rest]
        return done

    move(1)
    move(2)
    best = phase((), blocks, (), 8, diag=True)
    best = after(1, best)
    move(3)
    move(4)
    share(1)
    share(2)
    best = phase(FIRST, blocks, best, 8)
    best = phase(SECOND, blocks, best, 0)
    best = after(3, best)
    move(5)
    share(3)
    share(4)
    best = phase(THIRD, blocks, best, 8)
    best = after(5, best)
    *parts, lent = phase(LAST, blocks, best, 1, each=True)

    def give(i, part):
        back = tuple(minus((0, 0, 0), HELD[c][i]) for c in (0, 1))
        return lax.ppermute(part, AXES, moves(back))

    lent = lax.ppermute(lent, AXES, across())
    mine = jnp.maximum(parts[0], give(5, parts[5]))
    merged = pl.pallas_call(
        merge_kernel,
        out_shape=[jax.ShapeDtypeStruct((2, size), float32)] * len(SHARED),
        in_specs=[VMEM] * (len(SHARED) + 1),
        out_specs=[VMEM] * len(SHARED),
        compiler_params=pltpu.CompilerParams(vmem_limit_bytes=4 * 2**20),
    )(*[parts[i] for i in SHARED], lent)
    for i in (4, 3, 1, 2):
        mine = jnp.maximum(mine, give(i, merged[i - 1]))
    other = lax.ppermute(mine, AXES, across())
    return 1.0 - jnp.maximum(mine[:, :rows], other[:, rows:])


def solution(mesh):
    return jax.shard_map(
        shards,
        mesh=mesh,
        in_specs=(P(AXES, None), P()),
        out_specs=P(None, AXES),
        check_vma=False,
    )
```

```python
import functools
import itertools
import math

import jax
import jax.numpy as jnp
from jax import lax
from jax.experimental import pallas as pl
from jax.experimental.pallas import tpu as pltpu
from jax.sharding import PartitionSpec as P

AXES = ("row", "col")
SIDE = 4
HELD = (
    ((0, 0, 0), (0, 1, 1), (0, 0, 3), (3, 1, 1), (0, 0, 2), (3, 1, 2)),
    ((0, 0, 0), (3, 3, 0), (1, 0, 0), (3, 2, 0), (2, 0, 0), (2, 2, 0)),
)
SOURCE = (None, 0, 0, 1, 2, 3)
MOVED = 5
HALVED = (1, 3, 5)
SHARED = (1, 2, 3, 4)
FIRST = ((1, 0), (2, 0), (2, 1))
SECOND = ((1, 6), (2, 6), (2, 7))
THIRD = ((3, 0), (3, 1), (3, 2), (3, 6), (3, 7), (4, 0), (4, 7))
LAST = ((3, 8), (4, 8), (4, 9), (5, 1), (5, 4), (5, 6), (5, 7), (5, 9))
LOW = -3.0


def minus(a, b):
    return tuple((p - q) % SIDE for p, q in zip(a, b))


def coords(device):
    row, col = divmod(device, 16)
    y, x_lo = divmod(row, 2)
    return (col // 8 * 2 + x_lo, y, col // 2 % SIDE, col % 2)


def device_at(x, y, z, core):
    x, y, z = x % SIDE, y % SIDE, z % SIDE
    return (y * 2 + x % 2) * 16 + x // 2 * 8 + z * 2 + core


def moves(hops):
    out = []
    for target in range(128):
        x, y, z, core = coords(target)
        dx, dy, dz = hops[core]
        out.append((device_at(x + dx, y + dy, z + dz, core), target))
    return out


def across():
    return [(device, device ^ 1) for device in range(128)]


def offset_of(name, core):
    return HELD[core][name] if name <= MOVED else HELD[1 - core][name - MOVED]


def check_cover():
    seen = {(0, 0, 0)}
    for a, b in FIRST + SECOND + THIRD + LAST:
        for core in (0, 1):
            diff = minus(offset_of(a, core), offset_of(b, core))
            seen |= {diff, minus((0, 0, 0), diff)}
    assert seen == set(itertools.product(range(SIDE), repeat=3))


def may_touch(a, b):
    steps = {(0, 0, 1), (2, 0, 1), (3, 0, 1), (1, 1, 1)}
    steps |= {minus((0, 0, 0), step) for step in steps}
    return any(minus(offset_of(a, core), offset_of(b, core)) in steps for core in (0, 1))


def normalize(x):
    length = x.shape[1]
    average = jnp.sum(x, axis=1, keepdims=True) * (1.0 / length)
    centered = x - average
    power = jnp.sum(centered * centered, axis=1, keepdims=True) * (1.0 / length)
    spread_inv = lax.rsqrt(power + 1e-05) * (1.0 / math.sqrt(length))
    return (centered * spread_inv).astype(jnp.bfloat16)


def own_kernel(x_ref, o_ref):
    o_ref[...] = normalize(x_ref[...])


def both_kernel(own_ref, other_ref, half_ref, o_ref):
    rows = own_ref.shape[0]
    half = normalize(other_ref[...])
    half_ref[...] = half
    o_ref[:rows] = own_ref[...]
    o_ref[rows:] = half


def here():
    row, col = lax.axis_index("row"), lax.axis_index("col")
    x = (col >> 3) * 2 + (row & 1)
    return x, row >> 1, (col >> 1) & 3, col & 1


def order_of(name, place):
    x, y, z, core = place
    zero, one = offset_of(name, 0), offset_of(name, 1)
    sx, sy, sz = (
        (p + (a if a == b else jnp.where(core == 0, a, b))) & 3
        for p, a, b in zip((x, y, z), zero, one)
    )
    order = ((sy * 2 + (sx & 1)) * 2 + (sx >> 1)) * SIDE + sz
    return order, core if name <= MOVED else 1 - core


def positions(shape, dim, first, order, flip, size):
    at = lax.broadcasted_iota(jnp.int32, shape, dim) + (first + flip * (size // 2))
    return order * size + jnp.where(at >= size, at - size, at)


def phase_kernel(names, counts, pairs, diag, n_prev, each, *refs):
    exclude_ref = refs[0]
    rest = refs[1:]
    pieces = {}
    for name, count in zip(names, counts):
        pieces[name], rest = rest[:count], rest[count:]
    prev, rest = rest[:n_prev], rest[n_prev:]
    outs, (whole, row_acc, col_acc) = rest[:-3], rest[-3:]
    exclude = exclude_ref[0]
    place = here()
    size = whole.shape[1]
    blocks = {}
    for name, parts in pieces.items():
        if len(parts) == 1:
            blocks[name] = parts[0]
        else:
            blocks[name] = whole.at[sum(len(pieces[other]) > 1 for other in names if other < name)]
            for i, part in enumerate(parts):
                blocks[name][i * part.shape[0] : (i + 1) * part.shape[0]] = part[...]
    width = 256
    row_names = sorted({a for a, _ in pairs} | ({0} if diag else set()))
    col_names = sorted({b for _, b in pairs})

    row_acc[...] = jnp.full(row_acc.shape, LOW, jnp.float32)
    col_acc[...] = jnp.full(col_acc.shape, LOW, jnp.float32)

    def product(a, b, part):
        return lax.dot_general(
            blocks[a][...],
            blocks[b][part * width : (part + 1) * width],
            (((1,), (1,)), ((), ())),
            preferred_element_type=jnp.float32,
        )

    def row_max(values):
        best = values[:, :128]
        for at in range(128, width, 128):
            best = jnp.maximum(best, values[:, at : at + 128])
        return best

    def col_max(values):
        return jnp.max(values.reshape(size // 8, 8, width), axis=0)

    def apart(a, b, part):
        order_a, flip_a = order_of(a, place)
        order_b, flip_b = order_of(b, place)
        shape = (size, width)
        return positions(shape, 1, part * width, order_b, flip_b, size) - positions(
            shape, 0, 0, order_a, flip_a, size
        )

    def visit(a, b, masked):
        later = (order_of(b, place)[0] > order_of(a, place)[0]).astype(jnp.int32)
        row_at = 2 * row_names.index(a) + later
        col_at = 2 * col_names.index(b) + 1 - later
        for part in range(size // width):
            values = product(a, b, part)
            if masked:
                values = jnp.where(jnp.abs(apart(a, b, part)) > exclude, values, LOW)
            row_acc[row_at] = jnp.maximum(row_acc[row_at], row_max(values))
            at = pl.ds(part * width, width)
            col_acc[col_at, :, at] = jnp.maximum(col_acc[col_at, :, at], col_max(values))

    if diag:
        at = 2 * row_names.index(0)
        for part in range(size // width):
            values = product(0, 0, part)
            offset = apart(0, 0, part)
            earlier = jnp.where(offset < -exclude, values, LOW)
            later = jnp.where(offset > exclude, values, LOW)
            row_acc[at] = jnp.maximum(row_acc[at], row_max(earlier))
            row_acc[at + 1] = jnp.maximum(row_acc[at + 1], row_max(later))
    for a, b in pairs:
        if may_touch(a, b):
            near = jnp.abs(order_of(a, place)[0] - order_of(b, place)[0]) == 1
            pl.when(near)(functools.partial(visit, a, b, True))
            pl.when(jnp.logical_not(near))(functools.partial(visit, a, b, False))
        else:
            visit(a, b, False)

    lanes = lax.broadcasted_iota(jnp.int32, (size, 128), 1)
    gathered = jnp.full((size, 128), LOW, jnp.float32)
    for at in range(2 * len(row_names)):
        gathered = jnp.where(
            lanes == at, jnp.max(row_acc[at], axis=1, keepdims=True), gathered
        )
    turned = gathered.T
    folded = jnp.max(col_acc[...], axis=1)

    def result(name):
        parts = []
        if name in row_names:
            at = 2 * row_names.index(name)
            parts.append(turned[at : at + 2])
        if name in col_names:
            at = 2 * col_names.index(name)
            parts.append(folded[at : at + 2])
        if n_prev and name <= MOVED:
            parts.append(prev[0][2 * name : 2 * name + 2])
        elif n_prev:
            at = 2 * SHARED.index(name - MOVED)
            parts.append(prev[1][at : at + 2])
        return functools.reduce(jnp.maximum, parts) if parts else jnp.full((2, size), LOW)

    for name in range(MOVED + 1):
        if each:
            outs[name][...] = result(name)
        else:
            outs[0][2 * name : 2 * name + 2] = result(name)
    for i, name in enumerate(SHARED):
        outs[-1][2 * i : 2 * i + 2] = result(MOVED + name)


def merge_kernel(*refs):
    mine, other, outs = refs[: len(SHARED)], refs[len(SHARED)], refs[len(SHARED) + 1 :]
    for i in range(len(SHARED)):
        outs[i][...] = jnp.maximum(mine[i][...], other[2 * i : 2 * i + 2])


SMEM = pl.BlockSpec(memory_space=pltpu.SMEM)
VMEM = pl.BlockSpec(memory_space=pltpu.VMEM)


def shards(segments, exclusion):
    check_cover()
    rows, length = segments.shape
    size = 2 * rows
    float32 = jnp.float32

    def phase(pairs, blocks, prev, weight, diag=False, each=False):
        names = sorted({name for pair in pairs for name in pair} | ({0} if diag else set()))
        rows_of = {a for a, _ in pairs} | ({0} if diag else set())
        cols_of = {b for _, b in pairs}
        part = jax.ShapeDtypeStruct((2, size), float32)
        own_part = jax.ShapeDtypeStruct((2 * MOVED + 2, size), float32)
        out_shape = [part] * (MOVED + 1) if each else [own_part]
        out_shape.append(jax.ShapeDtypeStruct((2 * len(SHARED), size), float32))
        count = len(pairs) + diag
        counts = [len(blocks[name]) for name in names]
        return pl.pallas_call(
            functools.partial(
                phase_kernel, names, counts, pairs, diag, len(prev), each
            ),
            out_shape=out_shape,
            in_specs=[SMEM] + [VMEM] * (sum(counts) + len(prev)),
            out_specs=[VMEM] * len(out_shape),
            scratch_shapes=[
                pltpu.VMEM((max(1, sum(n > 1 for n in counts)), size, length), jnp.bfloat16),
                pltpu.VMEM((2 * len(rows_of), size, 128), float32),
                pltpu.VMEM((2 * max(len(cols_of), 1), 8, size), float32),
            ],
            compiler_params=pltpu.CompilerParams(vmem_limit_bytes=20 * 2**20),
            cost_estimate=pl.CostEstimate(
                flops=weight * 2 * count * size * size * length,
                bytes_accessed=2 * size * len(names),
                transcendentals=0,
            ),
        )(exclusion, *[part for name in names for part in blocks[name]], *prev)

    other = lax.ppermute(segments, AXES, across())
    own = pl.pallas_call(
        own_kernel,
        out_shape=jax.ShapeDtypeStruct((rows, length), jnp.bfloat16),
        in_specs=[VMEM],
        out_specs=VMEM,
        compiler_params=pltpu.CompilerParams(vmem_limit_bytes=8 * 2**20),
    )(segments)
    half, block = pl.pallas_call(
        both_kernel,
        out_shape=[
            jax.ShapeDtypeStruct((rows, length), jnp.bfloat16),
            jax.ShapeDtypeStruct((size, length), jnp.bfloat16),
        ],
        in_specs=[VMEM, VMEM],
        out_specs=[VMEM, VMEM],
        compiler_params=pltpu.CompilerParams(vmem_limit_bytes=8 * 2**20),
    )(own, other)

    blocks = {0: [block]}
    sources = {0: [own, half]}

    def move(i):
        hops = tuple(minus(HELD[c][i], HELD[c][SOURCE[i]]) for c in (0, 1))
        parts = sources.get(SOURCE[i], blocks[SOURCE[i]]) if i in HALVED else blocks[SOURCE[i]]
        blocks[i] = [lax.ppermute(part, AXES, moves(hops)) for part in parts]

    def share(i):
        blocks[MOVED + i] = [lax.ppermute(part, AXES, across()) for part in blocks[i]]

    def after(i, done):
        first, *rest = blocks[i]
        first, done = lax.optimization_barrier((first, done))
        blocks[i] = [first, *rest]
        return done

    move(1)
    move(2)
    best = phase((), blocks, (), 8, diag=True)
    best = after(1, best)
    move(3)
    move(4)
    share(1)
    share(2)
    best = phase(FIRST, blocks, best, 8)
    best = after(3, best)
    move(5)
    share(3)
    share(4)
    best = phase(SECOND + THIRD, blocks, best, 8)
    best = after(5, best)
    *parts, lent = phase(LAST, blocks, best, 1, each=True)

    def give(i, part):
        back = tuple(minus((0, 0, 0), HELD[c][i]) for c in (0, 1))
        return lax.ppermute(part, AXES, moves(back))

    lent = lax.ppermute(lent, AXES, across())
    mine = jnp.maximum(parts[0], give(5, parts[5]))
    merged = pl.pallas_call(
        merge_kernel,
        out_shape=[jax.ShapeDtypeStruct((2, size), float32)] * len(SHARED),
        in_specs=[VMEM] * (len(SHARED) + 1),
        out_specs=[VMEM] * len(SHARED),
        compiler_params=pltpu.CompilerParams(vmem_limit_bytes=4 * 2**20),
    )(*[parts[i] for i in SHARED], lent)
    for i in (4, 3, 1, 2):
        mine = jnp.maximum(mine, give(i, merged[i - 1]))
    other = lax.ppermute(mine, AXES, across())
    return 1.0 - jnp.maximum(mine[:, :rows], other[:, rows:])


def solution(mesh):
    return jax.shard_map(
        shards,
        mesh=mesh,
        in_specs=(P(AXES, None), P()),
        out_specs=P(None, AXES),
        check_vma=False,
    )
```
